32 devices in a mesh: leaf: 8 (over z, y), front: 4 (over x, core).
Axes of the slice: x: 2, y: 2, z: 4, core: 2. Of those that a mesh axis runs over, the one named last changes fastest.
Arguments:
- child_u: bfloat16 [131072, 128], P(('leaf', 'front')), may hold values from -6 to 6
- child_v: bfloat16 [131072, 128], P(('leaf', 'front')), may hold values from -0.59765625 to 0.59765625
- sketch: bfloat16 [3, 131072, 128], P(None, ('leaf', 'front')), may hold values from -6 to 6
- map_own: int32 [3, 131072], P(None, ('leaf', 'front')), may hold values from 0 to 4095
- map_peer: int32 [3, 131072], P(None, ('leaf', 'front')), may hold values from 0 to 4095
- live_rows: int32 [3, 32], P(None, ('leaf', 'front')), may hold values from 1 to 4096, 81920 in all within a row
- front_panel: bfloat16 [131072, 128], P(('leaf', 'front')), may hold values from -6 to 6
- pivot_inverse: bfloat16 [1024, 128], P('leaf'), may hold values from -0.5 to 0.5
Outputs:
- left_out: bfloat16 [131072, 128], P(('leaf', 'front'))
- right_out: bfloat16 [131072, 128], P(('leaf', 'front'))
- panel_out: bfloat16 [131072, 128], P(('leaf', 'front'))
The draws below stay inside these ranges and needn't reach their ends.
Inputs may be any that keep to these rules, and one draw needn't show every extreme that they name: `live_rows`: in each level every row of 32 counts sums to 81920, the largest being 4096 and the smallest at least 32.
All inputs are finite; a program needn't handle non-finite values. No bound on the sum of `live_rows` on one device may be relied on, other than what follows from the above.
Results may differ from the reference program's by a relative error of at most 0.01235.
Values may be sent and summed in bfloat16 or wider, within the bound.
A program may use at most 64 MiB of HBM per device.

```python
import math
import jax
import jax.numpy as jnp
import numpy as np
from jax import lax

R = 128
PW = 128
LEVELS = 3
ROWS = 4096
SLOTS = 32
TOTAL_ROWS = 131072
LIVE_SUM = 81920
PIVOT_ROWS = 1024
N_LEAF = 8
N_FRONT = 4


def touch_ends(array, key, least, high):
    index_at = [jax.random.randint(jax.random.fold_in(key, axis), (), 0, length) for axis, length in enumerate(array.shape)]
    main_axis = array.shape.index(max(array.shape))
    next_to = index_at[:main_axis] + [(index_at[main_axis] + 1) % array.shape[main_axis]] + index_at[main_axis + 1:]
    return array.at[tuple(index_at)].set(least).at[tuple(next_to)].set(high)


def steps_of(rng, shape, shards, smallest, high):
    gain, own = 1.0, jax.random.fold_in(rng, 6)
    for position, parts in shards:
        draws = jnp.exp(jax.random.uniform(jax.random.fold_in(own, position), (parts,), jnp.float32, smallest / len(shards), high / len(shards)))
        gain = gain * jnp.repeat(draws, shape[position] // parts).reshape([-1 if axis == position else 1 for axis in range(len(shape))])
    return gain


def profile(count, total, bound, skew):
    loads = [(1 << 20) // math.isqrt(grade ** skew) + 1 for grade in range(2, count + 1)]
    rest, counts = total - bound - (count - 1), [1] * (count - 1)
    while rest > 0:
        free = [i for i in range(count - 1) if counts[i] < bound]
        whole, left = sum([loads[i] for i in free]), rest
        for i in free:
            addition = min(bound - counts[i], max(1, left * loads[i] // whole), rest)
            counts[i] = counts[i] + addition
            rest = rest - addition
    return np.array([bound] + counts)


def uneven_parts(rng, amount, total, most, slope):
    if amount == 2:
        one = jax.random.randint(rng, (), max(1, total - most), min(most, total - 1) + 1)
        return jnp.stack([one, total - one])
    lengths = jnp.asarray(profile(amount, total, most, slope), jnp.int32)
    pairs = (amount - 1) // 2
    source_of, receiver = lengths[1:1 + 2 * pairs:2], lengths[2:2 + 2 * pairs:2]
    slack = jnp.minimum(source_of - 1, most - receiver)
    shifted = jax.random.randint(jax.random.fold_in(rng, 1), (pairs,), 0, 1 << 20) % (slack + 1)
    lengths = lengths.at[1:1 + 2 * pairs:2].set(source_of - shifted).at[2:2 + 2 * pairs:2].set(receiver + shifted)
    return lengths[jax.random.permutation(jax.random.fold_in(rng, 2), amount)]


def scatter_about(key, extent, width, most, pieces=(), kind=jnp.bfloat16):
    loudness = steps_of(key, extent, pieces, -0.22, 0.18) if pieces else 1.0
    entries = jax.random.normal(key, extent, jnp.float32) * width * loudness
    return jnp.minimum(jnp.maximum(entries, -most), most).astype(kind)


def setup_inputs(seed: int = 0) -> dict:
    splits = jax.random.split(jax.random.key(seed), 9)
    return {
        "child_u": scatter_about(splits[0], (TOTAL_ROWS, R), 1.0, 6.0, ((0, 32),)),
        "child_v": scatter_about(splits[1], (TOTAL_ROWS, R), 0.1, 0.59765625, ((0, 32),)),
        "sketch": scatter_about(splits[2], (LEVELS, TOTAL_ROWS, R), 1.0, 6.0, ((1, 32),)),
        "map_own": touch_ends(jax.random.randint(splits[3], (LEVELS, TOTAL_ROWS), 0, ROWS), jax.random.fold_in(splits[3], 1), 0, ROWS - 1).astype(jnp.int32),
        "map_peer": touch_ends(jax.random.randint(splits[4], (LEVELS, TOTAL_ROWS), 0, ROWS), jax.random.fold_in(splits[4], 1), 0, ROWS - 1).astype(jnp.int32),
        "live_rows": jax.vmap(lambda own: uneven_parts(own, SLOTS, LIVE_SUM, ROWS, 0))(jax.random.split(splits[5], LEVELS)).reshape((LEVELS, SLOTS)).astype(jnp.int32),
        "front_panel": scatter_about(splits[6], (TOTAL_ROWS, PW), 1.0, 6.0, ((0, 32),)),
        "pivot_inverse": scatter_about(splits[7], (PIVOT_ROWS, PW), PW ** -0.5, 0.5, ((0, 8),)),
    }


HIGHEST_PREC = lax.Precision.HIGHEST

def pick_rows(source, index):
    return jnp.take_along_axis(source, index[..., None], axis=2)

def reference(child_u, child_v, sketch, map_own, map_peer, live_rows, front_panel, pivot_inverse):
    left = child_u.reshape(N_LEAF, N_FRONT, ROWS, R)
    right = child_v.reshape(N_LEAF, N_FRONT, ROWS, R)
    row_index = jnp.arange(ROWS, dtype=jnp.int32)
    for tree_level in range(LEVELS):
        group_size = 2 ** (tree_level + 1)
        peer_index = np.arange(N_LEAF) ^ 2 ** tree_level
        map_self = map_own[tree_level].reshape(N_LEAF, N_FRONT, ROWS)
        map_other = map_peer[tree_level].reshape(N_LEAF, N_FRONT, ROWS)
        live = live_rows[tree_level].reshape(N_LEAF, N_FRONT)
        row_keep = (row_index[None, None, :] < live[:, :, None])[..., None]
        left_cat = jnp.concatenate([pick_rows(left, map_self), pick_rows(left[peer_index], map_other)], -1)
        right_cat = jnp.concatenate([pick_rows(right, map_self), pick_rows(right[peer_index], map_other)], -1)
        left_cat = jnp.where(row_keep, left_cat, 0).astype(jnp.bfloat16)
        right_cat = jnp.where(row_keep, right_cat, 0).astype(jnp.bfloat16)
        groups = N_LEAF // group_size
        span = group_size * N_FRONT * ROWS
        left_g = left_cat.reshape(groups, span, 2 * R).astype(jnp.float32)
        right_g = right_cat.reshape(groups, span, 2 * R).astype(jnp.float32)
        omega = sketch[tree_level].reshape(groups, span, R).astype(jnp.float32)
        sketch_b = jnp.einsum('gnr,gns->grs', right_g, omega, precision=HIGHEST_PREC)
        basis = jnp.einsum('gnr,grs->gns', left_g, sketch_b, precision=HIGHEST_PREC)
        gram = jnp.einsum('gnr,gns->grs', basis, basis, precision=HIGHEST_PREC)
        lower = jnp.linalg.cholesky(gram)
        ortho = lax.linalg.triangular_solve(lower, basis, left_side=False, lower=True, transpose_a=True)
        project = jnp.einsum('gnr,gns->grs', left_g, ortho, precision=HIGHEST_PREC)
        norm_scale = float(np.sqrt(span))
        left = (ortho * norm_scale).astype(jnp.bfloat16).reshape(N_LEAF, N_FRONT, ROWS, R)
        right_new = jnp.einsum('gnr,grs->gns', right_g, project, precision=HIGHEST_PREC)
        right = (right_new / norm_scale).astype(jnp.bfloat16).reshape(N_LEAF, N_FRONT, ROWS, R)
    right_piv = right[:, 0, :PW, :].astype(jnp.float32)
    panel_f = front_panel.reshape(N_LEAF, N_FRONT, ROWS, PW).astype(jnp.float32)
    updated = panel_f - jnp.einsum('lfnr,lpr->lfnp', left.astype(jnp.float32), right_piv, precision=HIGHEST_PREC)
    inverse_f = pivot_inverse.reshape(N_LEAF, PW, PW).astype(jnp.float32)
    panel_out = jnp.einsum('lfnp,lpq->lfnq', updated, inverse_f, precision=HIGHEST_PREC).astype(jnp.bfloat16)
    return (left.reshape(TOTAL_ROWS, R), right.reshape(TOTAL_ROWS, R), panel_out.reshape(TOTAL_ROWS, PW))
```

```python
import functools
import math

import jax
import jax.numpy as jnp
from jax import lax
from jax.experimental import pallas as pl
from jax.experimental.pallas import tpu as pltpu
from jax.sharding import PartitionSpec as P

BF16 = jnp.bfloat16
F32 = jnp.float32
HIGHEST_PREC = lax.Precision.HIGHEST
MESH = pl.DeviceIdType.MESH
VMEM_LIMIT = 48 * 1024 * 1024
UNROLL = 32
PIECE = 512

VMEM_SPEC = pl.BlockSpec(memory_space=pltpu.VMEM)
SMEM_SPEC = pl.BlockSpec(memory_space=pltpu.SMEM)


def from_partner(block, axis, stride):
    count = lax.axis_size(axis)
    route = []
    for low in range(count):
        high = low | 1 << stride
        if high != low and high < count:
            route += [(low, high), (high, low)]
    return lax.ppermute(block, axis, route)


def dot(first, second, dims=((1,), (0,)), precision=None):
    return lax.dot_general(
        first, second, (dims, ((), ())), preferred_element_type=F32, precision=precision
    )


def halves(wide):
    high = wide.astype(BF16)
    return high, (wide - high.astype(F32)).astype(BF16)


def gather_pairs(left_ref, right_ref, index_ref, live, table, picked):
    rows, width = left_ref.shape

    def fill(step, _):
        at = pl.multiple_of(step * PIECE, PIECE)
        table[pl.ds(2 * at, PIECE, stride=2), :] = left_ref[pl.ds(at, PIECE), :].astype(F32)
        table[pl.ds(2 * at + 1, PIECE, stride=2), :] = right_ref[pl.ds(at, PIECE), :].astype(F32)
        return 0

    lax.fori_loop(0, rows // PIECE, fill, 0)

    def pick(step, _):
        base = step * UNROLL
        loaded = []
        for j in range(UNROLL):
            loaded.append(table[pl.ds(2 * index_ref[base + j], 2), :])
        for j in range(UNROLL):
            picked[pl.ds(2 * (base + j), 2), :] = loaded[j]
        return 0

    lax.fori_loop(0, (live + UNROLL - 1) // UNROLL, pick, 0)


def read_pairs(picked, at, keep):
    first = picked[pl.ds(2 * at, PIECE, stride=2), :]
    second = picked[pl.ds(2 * at + 1, PIECE, stride=2), :]
    return jnp.where(keep, first, 0.0).astype(BF16), jnp.where(keep, second, 0.0).astype(BF16)


def keep_rows(at, live, width):
    return lax.broadcasted_iota(jnp.int32, (PIECE, width), 0) + at < live


def own_kernel(index_ref, live_ref, left_ref, right_ref, left_own, right_own, table, picked):
    rows, width = left_ref.shape
    live = live_ref[0, 0]
    gather_pairs(left_ref, right_ref, index_ref, live, table, picked)

    def store(step, _):
        at = pl.multiple_of(step * PIECE, PIECE)
        first, second = read_pairs(picked, at, keep_rows(at, live, width))
        left_own[pl.ds(at, PIECE), :] = first
        right_own[pl.ds(at, PIECE), :] = second
        return 0

    lax.fori_loop(0, rows // PIECE, store, 0)


def peer_kernel(
    index_ref, live_ref, left_ref, right_ref, left_own, right_own, sketch_ref,
    left_cat, right_cat, sums, table, picked,
):
    rows, width = left_ref.shape
    live = live_ref[0, 0]
    gather_pairs(left_ref, right_ref, index_ref, live, table, picked)
    sums[...] = jnp.zeros_like(sums)

    def add(step, _):
        at = pl.multiple_of(step * PIECE, PIECE)
        here = pl.ds(at, PIECE)
        first, second = read_pairs(picked, at, keep_rows(at, live, width))
        left_cat[here, :width] = left_own[here, :]
        left_cat[here, width:] = first
        right_cat[here, :width] = right_own[here, :]
        right_cat[here, width:] = second
        both = left_cat[here, :]
        gram = dot(both, both, ((0,), (0,)))
        sketched = dot(right_cat[here, :], sketch_ref[here, :], ((0,), (0,)))
        sums[: 2 * width, :] += sketched
        sums[2 * width : 3 * width, :] += gram[:width, :width]
        sums[3 * width : 4 * width, :] += gram[:width, width:]
        sums[4 * width : 5 * width, :] += gram[width:, width:]
        return 0

    lax.fori_loop(0, rows // PIECE, add, 0)


def inverse_factor(gram):
    size = gram.shape[0]
    tiles = [gram[8 * t : 8 * t + 8, :] for t in range(size // 8)]
    lane = lax.broadcasted_iota(jnp.int32, (8, size), 1)
    sublane = lax.broadcasted_iota(jnp.int32, (8, size), 0)
    pivots = [jnp.ones((8, size), F32) for _ in tiles]
    for k in range(size):
        own, within = divmod(k, 8)
        row = tiles[own][within : within + 1, :]
        pivot = row[:, k : k + 1]
        pivots[own] = jnp.where(sublane == within, pivot, pivots[own])
        scaled = row / pivot
        scaled = jnp.where(lane[:1] == k, 1.0 / pivot, scaled)
        for t in range(own, size // 8):
            column = tiles[t][:, k : k + 1]
            old = jnp.where(lane == k, 0.0, tiles[t])
            new = old - column * scaled
            if t == own:
                new = jnp.where(sublane > within, new, tiles[t])
                new = jnp.where((sublane == within) & (lane == k), 1.0, new)
            tiles[t] = new
    wide = [
        jnp.where(lane <= sublane + 8 * t, tile, 0.0) * lax.rsqrt(pivots[t])
        for t, tile in enumerate(tiles)
    ]
    return jnp.concatenate(wide, axis=0)


def front_kernel(
    level, pivot_rows, leaf_count, front_count,
    sums, left_cat, right_cat, *refs,
):
    last = pivot_rows > 0
    if last:
        panel, inverse, left_out, right_out, panel_out = refs[:5]
        parts, piece, total, pivots, send1, recv1, send2, recv2, send3, recv3 = refs[5:]
    else:
        left_out, right_out = refs[:2]
        parts, piece, total, send1, recv1, send2, recv2 = refs[2:]
    rows = left_cat.shape[0]
    width = left_cat.shape[1] // 2
    subtrees = 2 ** (level + 1)
    members = subtrees * front_count
    chunk = piece.shape[0]
    leaf, front = lax.axis_index("leaf"), lax.axis_index("front")
    low = lax.rem(leaf, subtrees)
    rank = low * front_count + front

    def device(place):
        return (leaf - low + place // front_count, lax.rem(place, front_count))

    barrier = pltpu.get_barrier_semaphore()

    def greet(d, _):
        pl.semaphore_signal(
            barrier, inc=1, device_id=device(lax.rem(rank + d, members)), device_id_type=MESH
        )
        return 0

    lax.fori_loop(1, members, greet, 0)
    pl.semaphore_wait(barrier, members - 1)

    def scatter(d):
        to = lax.rem(rank + d, members)
        return pltpu.make_async_remote_copy(
            src_ref=sums.at[pl.ds(pl.multiple_of(to * chunk, 8), chunk), :],
            dst_ref=parts.at[d],
            send_sem=send1.at[d],
            recv_sem=recv1.at[d],
            device_id=device(to),
            device_id_type=MESH,
        )

    mine = pl.ds(pl.multiple_of(rank * chunk, 8), chunk)

    def spread(d):
        to = lax.rem(rank + d, members)
        return pltpu.make_async_remote_copy(
            src_ref=piece,
            dst_ref=total.at[mine, :],
            send_sem=send2.at[d],
            recv_sem=recv2.at[d],
            device_id=device(to),
            device_id_type=MESH,
        )

    def start_pivots(d):
        return pltpu.make_async_remote_copy(
            src_ref=right_cat.at[pl.ds(0, pivot_rows), :],
            dst_ref=pivots.at[front],
            send_sem=send3.at[d],
            recv_sem=recv3.at[d],
            device_id=(leaf, lax.rem(front + d, front_count)),
            device_id_type=MESH,
        )

    def each(count, action):
        def body(d, _):
            action(d)
            return 0

        lax.fori_loop(1, count, body, 0)

    each(members, lambda d: scatter(d).start())
    if last:
        each(front_count, lambda d: start_pivots(d).start())
        pivots[front] = right_cat[:pivot_rows, :]
    piece[...] = sums[mine, :]

    def collect(d):
        scatter(d).wait_recv()
        piece[...] += parts[d]

    each(members, collect)
    each(members, lambda d: spread(d).start())
    total[mine, :] = piece[...]
    each(members, lambda d: spread(d).wait_recv())

    sketched = total[: 2 * width, :]
    cross = total[3 * width : 4 * width, :]
    upper = jnp.concatenate([total[2 * width : 3 * width, :], cross], axis=1)
    lower = jnp.concatenate([cross.T, total[4 * width : 5 * width, :]], axis=1)
    whole = jnp.concatenate([upper, lower], axis=0)
    applied = dot(whole, sketched, precision=HIGHEST_PREC)
    gram = dot(sketched, applied, ((0,), (0,)), precision=HIGHEST_PREC)
    inverted = inverse_factor(gram)
    scale = math.sqrt(members * rows)
    weights = dot(sketched, inverted, ((1,), (1,)), precision=HIGHEST_PREC)
    project = dot(applied, inverted, ((1,), (1,)), precision=HIGHEST_PREC)
    left_high, left_low = halves(weights * scale)
    right_high, right_low = halves(project / scale)

    if last:
        each(front_count, lambda d: start_pivots(d).wait_recv())
        first = pivots[0]
        right_piv = (dot(first, right_high) + dot(first, right_low)).astype(BF16)

    def out(step, _):
        here = pl.ds(pl.multiple_of(step * PIECE, PIECE), PIECE)
        left_rows = left_cat[here, :]
        right_rows = right_cat[here, :]
        left = (dot(left_rows, left_high) + dot(left_rows, left_low)).astype(BF16)
        left_out[here, :] = left
        right_out[here, :] = (dot(right_rows, right_high) + dot(right_rows, right_low)).astype(BF16)
        if last:
            updated = panel[here, :].astype(F32) - dot(left, right_piv, ((1,), (1,)))
            high, rest = halves(updated)
            panel_out[here, :] = (dot(high, inverse[...]) + dot(rest, inverse[...])).astype(BF16)
        return 0

    lax.fori_loop(0, rows // PIECE, out, 0)
    each(members, lambda d: scatter(d).wait_send())
    each(members, lambda d: spread(d).wait_send())
    if last:
        each(front_count, lambda d: start_pivots(d).wait_send())


def params(**more):
    return pltpu.CompilerParams(vmem_limit_bytes=VMEM_LIMIT, **more)


def on_device(child_u, child_v, sketch, map_own, map_peer, live_rows, front_panel, pivot_inverse):
    rows, width = child_u.shape
    level_count = sketch.shape[0]
    front_count = lax.axis_size("front")
    leaf_count = lax.axis_size("leaf")
    left, right = child_u, child_v
    narrow = jax.ShapeDtypeStruct((rows, width), BF16)
    cat = jax.ShapeDtypeStruct((rows, 2 * width), BF16)
    tables = [pltpu.VMEM((2 * rows, width), F32)] * 2
    for level in range(level_count):
        members = 2 ** (level + 1) * front_count
        chunk = -(-5 * width // (8 * members)) * 8
        live = live_rows[level].reshape(1, 1)
        left_sibling = from_partner(left, "leaf", level)
        right_sibling = from_partner(right, "leaf", level)
        with jax.named_scope("own_rows"):
            left_own, right_own = pl.pallas_call(
                own_kernel,
                out_shape=(narrow, narrow),
                in_specs=[SMEM_SPEC] * 2 + [VMEM_SPEC] * 2,
                out_specs=(VMEM_SPEC,) * 2,
                scratch_shapes=tables,
                compiler_params=params(),
                cost_estimate=pl.CostEstimate(
                    flops=10 * rows * width, bytes_accessed=20 * rows * width, transcendentals=0
                ),
            )(map_own[level], live, left, right)
        with jax.named_scope("peer_rows"):
            left_cat, right_cat, sums = pl.pallas_call(
                peer_kernel,
                out_shape=(cat, cat, jax.ShapeDtypeStruct((members * chunk, width), F32)),
                in_specs=[SMEM_SPEC] * 2 + [VMEM_SPEC] * 5,
                out_specs=(VMEM_SPEC,) * 3,
                scratch_shapes=tables,
                compiler_params=params(),
                cost_estimate=pl.CostEstimate(
                    flops=12 * rows * width * width, bytes_accessed=20 * rows * width,
                    transcendentals=0,
                ),
            )(
                map_peer[level], live, left_sibling, right_sibling, left_own, right_own,
                sketch[level],
            )
        last = level == level_count - 1
        operands = [sums, left_cat, right_cat]
        outs = [narrow, narrow]
        scratch = [
            pltpu.VMEM((members, chunk, width), F32),
            pltpu.VMEM((chunk, width), F32),
            pltpu.VMEM((members * chunk, width), F32),
        ]
        if last:
            operands += [front_panel, pivot_inverse]
            outs += [jax.ShapeDtypeStruct(front_panel.shape, BF16)]
            scratch += [pltpu.VMEM((front_count, pivot_inverse.shape[0], 2 * width), BF16)]
        scratch += [pltpu.SemaphoreType.DMA((members,))] * 4
        if last:
            scratch += [pltpu.SemaphoreType.DMA((front_count,))] * 2
        with jax.named_scope("group_sum_and_fronts"):
            results = pl.pallas_call(
                functools.partial(
                    front_kernel, level, pivot_inverse.shape[0] if last else 0,
                    leaf_count, front_count,
                ),
                out_shape=tuple(outs),
                in_specs=[VMEM_SPEC] * len(operands),
                out_specs=(VMEM_SPEC,) * len(outs),
                scratch_shapes=scratch,
                compiler_params=params(collective_id=level, has_side_effects=True),
                cost_estimate=pl.CostEstimate(
                    flops=16 * rows * width * width, bytes_accessed=20 * rows * width,
                    transcendentals=0,
                ),
            )(*operands)
        left, right = results[:2]
    return left, right, results[2]


def solution(mesh):
    placed = (
        P(("leaf", "front"), None),
        P(("leaf", "front"), None),
        P(None, ("leaf", "front"), None),
        P(None, ("leaf", "front")),
        P(None, ("leaf", "front")),
        P(None, ("leaf", "front")),
        P(("leaf", "front"), None),
        P("leaf", None),
    )
    return jax.shard_map(
        on_device,
        mesh=mesh,
        in_specs=placed,
        out_specs=(
            P(("leaf", "front"), None),
            P(("leaf", "front"), None),
            P(("leaf", "front"), None),
        ),
        check_vma=False,
    )
```

```python
import functools
import math

import jax
import jax.numpy as jnp
from jax import lax
from jax.experimental import pallas as pl
from jax.experimental.pallas import tpu as pltpu
from jax.sharding import PartitionSpec as P

BF16 = jnp.bfloat16
F32 = jnp.float32
HIGHEST_PREC = lax.Precision.HIGHEST
MESH = pl.DeviceIdType.MESH
VMEM_LIMIT = 48 * 1024 * 1024
UNROLL = 32
PIECE = 512

VMEM_SPEC = pl.BlockSpec(memory_space=pltpu.VMEM)
SMEM_SPEC = pl.BlockSpec(memory_space=pltpu.SMEM)


def from_partner(block, axis, stride):
    count = lax.axis_size(axis)
    route = []
    for low in range(count):
        high = low | 1 << stride
        if high != low and high < count:
            route += [(low, high), (high, low)]
    return lax.ppermute(block, axis, route)


def dot(first, second, dims=((1,), (0,)), precision=None):
    return lax.dot_general(
        first, second, (dims, ((), ())), preferred_element_type=F32, precision=precision
    )


def halves(wide):
    high = wide.astype(BF16)
    return high, (wide - high.astype(F32)).astype(BF16)


def fill_pairs(left_ref, right_ref, table):
    def fill(step, _):
        at = pl.multiple_of(step * PIECE, PIECE)
        table[pl.ds(2 * at, PIECE, stride=2), :] = left_ref[pl.ds(at, PIECE), :].astype(F32)
        table[pl.ds(2 * at + 1, PIECE, stride=2), :] = right_ref[pl.ds(at, PIECE), :].astype(F32)
        return 0

    lax.fori_loop(0, left_ref.shape[0] // PIECE, fill, 0)


def fill_single(source_ref, table):
    def fill(step, _):
        here = pl.ds(pl.multiple_of(step * PIECE, PIECE), PIECE)
        table[here, :] = source_ref[here, :].astype(F32)
        return 0

    lax.fori_loop(0, source_ref.shape[0] // PIECE, fill, 0)


def pick_rows(index_ref, live, table, picked, wide):
    def pick(step, _):
        base = step * UNROLL
        loaded = []
        for j in range(UNROLL):
            loaded.append(table[pl.ds(wide * index_ref[base + j], wide), :])
        for j in range(UNROLL):
            picked[pl.ds(wide * (base + j), wide), :] = loaded[j]
        return 0

    lax.fori_loop(0, (live + UNROLL - 1) // UNROLL, pick, 0)


def keep_rows(at, live, width):
    return lax.broadcasted_iota(jnp.int32, (PIECE, width), 0) + at < live


def pieces(rows, action):
    def body(step, _):
        action(pl.multiple_of(step * PIECE, PIECE))
        return 0

    lax.fori_loop(0, rows // PIECE, body, 0)


def own_kernel(index_ref, live_ref, left_ref, right_ref, left_own, right_own, table, picked):
    rows, width = left_ref.shape
    live = live_ref[0, 0]
    fill_pairs(left_ref, right_ref, table)
    pick_rows(index_ref, live, table, picked, 2)

    def store(at):
        keep = keep_rows(at, live, width)
        here = pl.ds(at, PIECE)
        first = picked[pl.ds(2 * at, PIECE, stride=2), :]
        second = picked[pl.ds(2 * at + 1, PIECE, stride=2), :]
        left_own[here, :] = jnp.where(keep, first, 0.0).astype(BF16)
        right_own[here, :] = jnp.where(keep, second, 0.0).astype(BF16)

    pieces(rows, store)


def sketch_kernel(
    other_ref, right_ref, right_own, sketch_ref, other_sketch, sums, table, picked
):
    rows, width = right_ref.shape
    live = other_ref[rows]
    fill_single(right_ref, table)
    pick_rows(other_ref, live, table, picked, 1)
    sums[...] = jnp.zeros_like(sums)

    def add(at):
        here = pl.ds(at, PIECE)
        sums[:width, :] += dot(right_own[here, :], sketch_ref[here, :], ((0,), (0,)))
        given = jnp.where(keep_rows(at, live, width), picked[here, :], 0.0).astype(BF16)
        sums[width:, :] += dot(given, other_sketch[here, :], ((0,), (0,)))

    pieces(rows, add)


def left_kernel(index_ref, live_ref, left_ref, left_own, left_cat, sums, table, picked):
    rows, width = left_ref.shape
    live = live_ref[0, 0]
    fill_single(left_ref, table)
    pick_rows(index_ref, live, table, picked, 1)
    sums[...] = jnp.zeros_like(sums)

    def add(at):
        here = pl.ds(at, PIECE)
        given = jnp.where(keep_rows(at, live, width), picked[here, :], 0.0).astype(BF16)
        left_cat[here, :width] = left_own[here, :]
        left_cat[here, width:] = given
        both = left_cat[here, :]
        gram = dot(both, both, ((0,), (0,)))
        sums[:width, :] += gram[:width, :width]
        sums[width : 2 * width, :] += gram[:width, width:]
        sums[2 * width :, :] += gram[width:, width:]

    pieces(rows, add)


def right_kernel(
    index_ref, live_ref, right_ref, right_own, project_high, project_low, right_out, table, picked
):
    rows, width = right_ref.shape
    live = live_ref[0, 0]
    fill_single(right_ref, table)
    pick_rows(index_ref, live, table, picked, 1)

    def out(at):
        here = pl.ds(at, PIECE)
        given = jnp.where(keep_rows(at, live, width), picked[here, :], 0.0).astype(BF16)
        both = jnp.concatenate([right_own[here, :], given], axis=1)
        right_out[here, :] = (dot(both, project_high[...]) + dot(both, project_low[...])).astype(BF16)

    pieces(rows, out)


def inverse_factor(gram):
    size = gram.shape[0]
    tiles = [gram[8 * t : 8 * t + 8, :] for t in range(size // 8)]
    lane = lax.broadcasted_iota(jnp.int32, (8, size), 1)
    sublane = lax.broadcasted_iota(jnp.int32, (8, size), 0)
    pivots = [jnp.ones((8, size), F32) for _ in tiles]
    for k in range(size):
        own, within = divmod(k, 8)
        row = tiles[own][within : within + 1, :]
        pivot = row[:, k : k + 1]
        pivots[own] = jnp.where(sublane == within, pivot, pivots[own])
        inverse = 1.0 / pivot
        scaled = jnp.where(lane[:1] == k, inverse, row * inverse)
        for t in range(own, size // 8):
            column = tiles[t][:, k : k + 1]
            old = jnp.where(lane == k, 0.0, tiles[t])
            new = old - column * scaled
            if t == own:
                new = jnp.where(sublane > within, new, tiles[t])
                new = jnp.where((sublane == within) & (lane == k), 1.0, new)
            tiles[t] = new
    wide = [
        jnp.where(lane <= sublane + 8 * t, tile, 0.0) * lax.rsqrt(pivots[t])
        for t, tile in enumerate(tiles)
    ]
    return jnp.concatenate(wide, axis=0)


def greet(peers):
    barrier = pltpu.get_barrier_semaphore()
    count = peers[0]

    def signal(d, _):
        pl.semaphore_signal(barrier, inc=1, device_id=peers[1](d), device_id_type=MESH)
        return 0

    lax.fori_loop(1, count, signal, 0)
    pl.semaphore_wait(barrier, count - 1)


def each(count, action):
    def body(d, _):
        action(d)
        return 0

    lax.fori_loop(1, count, body, 0)


def factor_kernel(
    level, front_count, sketch_sums, gram_sums, left_cat, left_out, project_high, project_low,
    local, parts, piece, total, send1, recv1, send2, recv2,
):
    rows = left_cat.shape[0]
    width = left_cat.shape[1] // 2
    subtrees = 2 ** (level + 1)
    members = subtrees * front_count
    chunk = piece.shape[0]
    leaf, front = lax.axis_index("leaf"), lax.axis_index("front")
    low = lax.rem(leaf, subtrees)
    rank = low * front_count + front

    def device(d):
        place = lax.rem(rank + d, members)
        return (leaf - low + place // front_count, lax.rem(place, front_count))

    local[: 2 * width, :] = sketch_sums[...]
    local[2 * width : 5 * width, :] = gram_sums[...]
    if local.shape[0] > 5 * width:
        local[5 * width :, :] = jnp.zeros((local.shape[0] - 5 * width, width), F32)
    greet((members, device))

    def scatter(d):
        to = lax.rem(rank + d, members)
        return pltpu.make_async_remote_copy(
            src_ref=local.at[pl.ds(pl.multiple_of(to * chunk, 8), chunk), :],
            dst_ref=parts.at[d],
            send_sem=send1.at[d],
            recv_sem=recv1.at[d],
            device_id=device(d),
            device_id_type=MESH,
        )

    mine = pl.ds(pl.multiple_of(rank * chunk, 8), chunk)

    def spread(d):
        return pltpu.make_async_remote_copy(
            src_ref=piece,
            dst_ref=total.at[mine, :],
            send_sem=send2.at[d],
            recv_sem=recv2.at[d],
            device_id=device(d),
            device_id_type=MESH,
        )

    each(members, lambda d: scatter(d).start())
    piece[...] = local[mine, :]

    def collect(d):
        scatter(d).wait_recv()
        piece[...] += parts[d]

    each(members, collect)
    each(members, lambda d: spread(d).start())
    total[mine, :] = piece[...]
    each(members, lambda d: spread(d).wait_recv())

    sketched = total[: 2 * width, :]
    cross = total[3 * width : 4 * width, :]
    upper = jnp.concatenate([total[2 * width : 3 * width, :], cross], axis=1)
    lower = jnp.concatenate([cross.T, total[4 * width : 5 * width, :]], axis=1)
    whole = jnp.concatenate([upper, lower], axis=0)
    applied = dot(whole, sketched, precision=HIGHEST_PREC)
    gram = dot(sketched, applied, ((0,), (0,)), precision=HIGHEST_PREC)
    inverted = inverse_factor(gram)
    scale = math.sqrt(members * rows)
    weights = dot(sketched, inverted, ((1,), (1,)), precision=HIGHEST_PREC)
    left_high, left_low = halves(weights * scale)

    def out(at):
        here = pl.ds(at, PIECE)
        left_rows = left_cat[here, :]
        left_out[here, :] = (dot(left_rows, left_high) + dot(left_rows, left_low)).astype(BF16)

    pieces(rows, out)
    project = dot(applied, inverted, ((1,), (1,)), precision=HIGHEST_PREC)
    high, rest = halves(project / scale)
    project_high[...] = high
    project_low[...] = rest
    each(members, lambda d: scatter(d).wait_send())
    each(members, lambda d: spread(d).wait_send())


def panel_kernel(front_count, left, right, panel, inverse, panel_out, pivots, send, recv):
    leaf, front = lax.axis_index("leaf"), lax.axis_index("front")
    pivot_rows = inverse.shape[0]

    def device(d):
        return (leaf, lax.rem(front + d, front_count))

    greet((front_count, device))

    def share(d):
        return pltpu.make_async_remote_copy(
            src_ref=right.at[pl.ds(0, pivot_rows), :],
            dst_ref=pivots.at[front],
            send_sem=send.at[d],
            recv_sem=recv.at[d],
            device_id=device(d),
            device_id_type=MESH,
        )

    each(front_count, lambda d: share(d).start())
    pivots[front] = right[:pivot_rows, :]
    each(front_count, lambda d: share(d).wait_recv())
    right_piv = pivots[0]

    def out(at):
        here = pl.ds(at, PIECE)
        updated = panel[here, :].astype(F32) - dot(left[here, :], right_piv, ((1,), (1,)))
        high, rest = halves(updated)
        panel_out[here, :] = (dot(high, inverse[...]) + dot(rest, inverse[...])).astype(BF16)

    pieces(left.shape[0], out)
    each(front_count, lambda d: share(d).wait_send())


def call(kernel, outs, operands, scalars, scratch, flops, moved, **more):
    return pl.pallas_call(
        kernel,
        out_shape=outs,
        in_specs=[SMEM_SPEC] * scalars + [VMEM_SPEC] * (len(operands) - scalars),
        out_specs=tuple(VMEM_SPEC for _ in outs),
        scratch_shapes=scratch,
        compiler_params=pltpu.CompilerParams(vmem_limit_bytes=VMEM_LIMIT, **more),
        cost_estimate=pl.CostEstimate(flops=flops, bytes_accessed=moved, transcendentals=0),
    )(*operands)


def on_device(child_u, child_v, sketch, map_own, map_peer, live_rows, front_panel, pivot_inverse):
    rows, width = child_u.shape
    level_count = sketch.shape[0]
    front_count = lax.axis_size("front")
    left, right = child_u, child_v
    narrow = jax.ShapeDtypeStruct((rows, width), BF16)
    cat = jax.ShapeDtypeStruct((rows, 2 * width), BF16)
    small = jax.ShapeDtypeStruct((2 * width, width), BF16)
    pairs = [pltpu.VMEM((2 * rows, width), F32)] * 2
    singles = [pltpu.VMEM((rows, width), F32)] * 2
    unit = 22_000_000
    others = []
    for level in range(level_count):
        tail = jnp.broadcast_to(live_rows[level], (width,))
        others.append(from_partner(jnp.concatenate([map_peer[level], tail]), "leaf", level))
    left_sibling = from_partner(left, "leaf", 0)
    other_sketch = [from_partner(sketch[level], "leaf", level) for level in range(level_count)]
    for level in range(level_count):
        members = 2 ** (level + 1) * front_count
        chunk = -(-5 * width // (8 * members)) * 8
        live = live_rows[level].reshape(1, 1)
        if level:
            left_sibling = from_partner(left, "leaf", level)
        right_sibling = from_partner(right, "leaf", level)
        with jax.named_scope("own_rows"):
            left_own, right_own = call(
                own_kernel, (narrow, narrow), [map_own[level], live, left, right], 2, pairs,
                rows * width, unit,
            )
        with jax.named_scope("sketch_sums"):
            (sketch_sums,) = call(
                sketch_kernel, (jax.ShapeDtypeStruct((2 * width, width), F32),),
                [others[level], right, right_own, sketch[level], other_sketch[level]],
                1, singles, 4 * rows * width * width, unit,
            )
        with jax.named_scope("left_rows"):
            left_cat, gram_sums = call(
                left_kernel, (cat, jax.ShapeDtypeStruct((3 * width, width), F32)),
                [map_peer[level], live, left_sibling, left_own], 2, singles,
                8 * rows * width * width, unit,
            )
        if level == 0:
            (gram_sums, sketch_sums), others[2:], other_sketch[2:] = lax.optimization_barrier(
                ((gram_sums, sketch_sums), others[2:], other_sketch[2:])
            )
        with jax.named_scope("group_sum_and_factor"):
            left, project_high, project_low = call(
                functools.partial(factor_kernel, level, front_count),
                (narrow, small, small), [sketch_sums, gram_sums, left_cat], 0,
                [
                    pltpu.VMEM((members * chunk, width), F32),
                    pltpu.VMEM((members, chunk, width), F32),
                    pltpu.VMEM((chunk, width), F32),
                    pltpu.VMEM((members * chunk, width), F32),
                ]
                + [pltpu.SemaphoreType.DMA((members,))] * 4,
                8 * rows * width * width, 4 * unit,
                collective_id=level, has_side_effects=True,
            )
        if level == 0:
            (left, project_high), others[1:], other_sketch[1:] = lax.optimization_barrier(
                ((left, project_high), others[1:], other_sketch[1:])
            )
        with jax.named_scope("right_rows"):
            (right,) = call(
                right_kernel, (narrow,),
                [map_peer[level], live, right_sibling, right_own, project_high, project_low],
                2, singles, 8 * rows * width * width, unit,
            )
    with jax.named_scope("panel"):
        (panel_out,) = call(
            functools.partial(panel_kernel, front_count),
            (jax.ShapeDtypeStruct(front_panel.shape, BF16),),
            [left, right, front_panel, pivot_inverse], 0,
            [pltpu.VMEM((front_count,) + pivot_inverse.shape, BF16)]
            + [pltpu.SemaphoreType.DMA((front_count,))] * 2,
            8 * rows * width * width, unit,
            collective_id=level_count, has_side_effects=True,
        )
    return left, right, panel_out


def solution(mesh):
    placed = (
        P(("leaf", "front"), None),
        P(("leaf", "front"), None),
        P(None, ("leaf", "front"), None),
        P(None, ("leaf", "front")),
        P(None, ("leaf", "front")),
        P(None, ("leaf", "front")),
        P(("leaf", "front"), None),
        P("leaf", None),
    )
    return jax.shard_map(
        on_device,
        mesh=mesh,
        in_specs=placed,
        out_specs=(
            P(("leaf", "front"), None),
            P(("leaf", "front"), None),
            P(("leaf", "front"), None),
        ),
        check_vma=False,
    )
```

```python
import functools
import math

import jax
import jax.numpy as jnp
from jax import lax
from jax.experimental import pallas as pl
from jax.experimental.pallas import tpu as pltpu
from jax.sharding import PartitionSpec as P

BF16 = jnp.bfloat16
F32 = jnp.float32
HIGHEST_PREC = lax.Precision.HIGHEST
MESH = pl.DeviceIdType.MESH
VMEM_LIMIT = 48 * 1024 * 1024
UNROLL = 32
PIECE = 512

VMEM_SPEC = pl.BlockSpec(memory_space=pltpu.VMEM)
SMEM_SPEC = pl.BlockSpec(memory_space=pltpu.SMEM)


def from_partner(block, axis, stride):
    count = lax.axis_size(axis)
    route = []
    for low in range(count):
        high = low | 1 << stride
        if high != low and high < count:
            route += [(low, high), (high, low)]
    return lax.ppermute(block, axis, route)


def dot(first, second, dims=((1,), (0,)), precision=None):
    return lax.dot_general(
        first, second, (dims, ((), ())), preferred_element_type=F32, precision=precision
    )


def halves(wide):
    high = wide.astype(BF16)
    return high, (wide - high.astype(F32)).astype(BF16)


def fill_pairs(left_ref, right_ref, table):
    def fill(step, _):
        at = pl.multiple_of(step * PIECE, PIECE)
        table[pl.ds(2 * at, PIECE, stride=2), :] = left_ref[pl.ds(at, PIECE), :].astype(F32)
        table[pl.ds(2 * at + 1, PIECE, stride=2), :] = right_ref[pl.ds(at, PIECE), :].astype(F32)
        return 0

    lax.fori_loop(0, left_ref.shape[0] // PIECE, fill, 0)


def fill_single(source_ref, table):
    def fill(step, _):
        here = pl.ds(pl.multiple_of(step * PIECE, PIECE), PIECE)
        table[here, :] = source_ref[here, :].astype(F32)
        return 0

    lax.fori_loop(0, source_ref.shape[0] // PIECE, fill, 0)


def pick_rows(index_ref, live, table, picked, wide):
    def pick(step, _):
        base = step * UNROLL
        loaded = []
        for j in range(UNROLL):
            loaded.append(table[pl.ds(wide * index_ref[base + j], wide), :])
        for j in range(UNROLL):
            picked[pl.ds(wide * (base + j), wide), :] = loaded[j]
        return 0

    lax.fori_loop(0, (live + UNROLL - 1) // UNROLL, pick, 0)


def keep_rows(at, live, width):
    return lax.broadcasted_iota(jnp.int32, (PIECE, width), 0) + at < live


def pieces(rows, action):
    def body(step, _):
        action(pl.multiple_of(step * PIECE, PIECE))
        return 0

    lax.fori_loop(0, rows // PIECE, body, 0)


def own_kernel(index_ref, live_ref, left_ref, right_ref, left_own, right_own, table, picked):
    rows, width = left_ref.shape
    live = live_ref[0, 0]
    fill_pairs(left_ref, right_ref, table)
    pick_rows(index_ref, live, table, picked, 2)

    def store(at):
        keep = keep_rows(at, live, width)
        here = pl.ds(at, PIECE)
        first = picked[pl.ds(2 * at, PIECE, stride=2), :]
        second = picked[pl.ds(2 * at + 1, PIECE, stride=2), :]
        left_own[here, :] = jnp.where(keep, first, 0.0).astype(BF16)
        right_own[here, :] = jnp.where(keep, second, 0.0).astype(BF16)

    pieces(rows, store)


def sketch_kernel(
    other_ref, right_ref, right_own, sketch_ref, other_sketch, sums, table, picked
):
    rows, width = right_ref.shape
    live = other_ref[rows]
    fill_single(right_ref, table)
    pick_rows(other_ref, live, table, picked, 1)
    sums[...] = jnp.zeros_like(sums)

    def add(at):
        here = pl.ds(at, PIECE)
        sums[:width, :] += dot(right_own[here, :], sketch_ref[here, :], ((0,), (0,)))
        given = jnp.where(keep_rows(at, live, width), picked[here, :], 0.0).astype(BF16)
        sums[width:, :] += dot(given, other_sketch[here, :], ((0,), (0,)))

    pieces(rows, add)


def left_kernel(index_ref, live_ref, left_ref, left_own, left_cat, sums, table, picked):
    rows, width = left_ref.shape
    live = live_ref[0, 0]
    fill_single(left_ref, table)
    pick_rows(index_ref, live, table, picked, 1)
    sums[...] = jnp.zeros_like(sums)

    def add(at):
        here = pl.ds(at, PIECE)
        given = jnp.where(keep_rows(at, live, width), picked[here, :], 0.0).astype(BF16)
        left_cat[here, :width] = left_own[here, :]
        left_cat[here, width:] = given
        both = left_cat[here, :]
        gram = dot(both, both, ((0,), (0,)))
        sums[:width, :] += gram[:width, :width]
        sums[width : 2 * width, :] += gram[:width, width:]
        sums[2 * width :, :] += gram[width:, width:]

    pieces(rows, add)


def right_kernel(
    index_ref, live_ref, right_ref, right_own, project_high, project_low, right_out, table, picked
):
    rows, width = right_ref.shape
    live = live_ref[0, 0]
    fill_single(right_ref, table)
    pick_rows(index_ref, live, table, picked, 1)

    def out(at):
        here = pl.ds(at, PIECE)
        given = jnp.where(keep_rows(at, live, width), picked[here, :], 0.0).astype(BF16)
        both = jnp.concatenate([right_own[here, :], given], axis=1)
        right_out[here, :] = (dot(both, project_high[...]) + dot(both, project_low[...])).astype(BF16)

    pieces(rows, out)


def inverse_factor(gram):
    size = gram.shape[0]
    tiles = [gram[8 * t : 8 * t + 8, :] for t in range(size // 8)]
    lane = lax.broadcasted_iota(jnp.int32, (8, size), 1)
    sublane = lax.broadcasted_iota(jnp.int32, (8, size), 0)
    pivots = [jnp.ones((8, size), F32) for _ in tiles]
    for k in range(size):
        own, within = divmod(k, 8)
        row = tiles[own][within : within + 1, :]
        pivot = row[:, k : k + 1]
        pivots[own] = jnp.where(sublane == within, pivot, pivots[own])
        inverse = 1.0 / pivot
        scaled = jnp.where(lane[:1] == k, inverse, row * inverse)
        for t in range(own, size // 8):
            column = tiles[t][:, k : k + 1]
            old = jnp.where(lane == k, 0.0, tiles[t])
            new = old - column * scaled
            if t == own:
                new = jnp.where(sublane > within, new, tiles[t])
                new = jnp.where((sublane == within) & (lane == k), 1.0, new)
            tiles[t] = new
    wide = [
        jnp.where(lane <= sublane + 8 * t, tile, 0.0) * lax.rsqrt(pivots[t])
        for t, tile in enumerate(tiles)
    ]
    return jnp.concatenate(wide, axis=0)


def greet(peers):
    barrier = pltpu.get_barrier_semaphore()
    count = peers[0]

    def signal(d, _):
        pl.semaphore_signal(barrier, inc=1, device_id=peers[1](d), device_id_type=MESH)
        return 0

    lax.fori_loop(1, count, signal, 0)
    pl.semaphore_wait(barrier, count - 1)


def each(count, action):
    def body(d, _):
        action(d)
        return 0

    lax.fori_loop(1, count, body, 0)


def factor_kernel(
    level, front_count, sketch_sums, gram_sums, left_cat, left_out, project_high, project_low,
    local, parts, piece, total, send1, recv1, send2, recv2,
):
    rows = left_cat.shape[0]
    width = left_cat.shape[1] // 2
    subtrees = 2 ** (level + 1)
    members = subtrees * front_count
    chunk = piece.shape[0]
    leaf, front = lax.axis_index("leaf"), lax.axis_index("front")
    low = lax.rem(leaf, subtrees)
    rank = low * front_count + front

    def device(d):
        place = lax.rem(rank + d, members)
        return (leaf - low + place // front_count, lax.rem(place, front_count))

    local[: 2 * width, :] = sketch_sums[...]
    local[2 * width : 5 * width, :] = gram_sums[...]
    if local.shape[0] > 5 * width:
        local[5 * width :, :] = jnp.zeros((local.shape[0] - 5 * width, width), F32)
    greet((members, device))

    def scatter(d):
        to = lax.rem(rank + d, members)
        return pltpu.make_async_remote_copy(
            src_ref=local.at[pl.ds(pl.multiple_of(to * chunk, 8), chunk), :],
            dst_ref=parts.at[d],
            send_sem=send1.at[d],
            recv_sem=recv1.at[d],
            device_id=device(d),
            device_id_type=MESH,
        )

    mine = pl.ds(pl.multiple_of(rank * chunk, 8), chunk)

    def spread(d):
        return pltpu.make_async_remote_copy(
            src_ref=piece,
            dst_ref=total.at[mine, :],
            send_sem=send2.at[d],
            recv_sem=recv2.at[d],
            device_id=device(d),
            device_id_type=MESH,
        )

    each(members, lambda d: scatter(d).start())
    piece[...] = local[mine, :]

    def collect(d):
        scatter(d).wait_recv()
        piece[...] += parts[d]

    each(members, collect)
    each(members, lambda d: spread(d).start())
    total[mine, :] = piece[...]
    each(members, lambda d: spread(d).wait_recv())

    sketched = total[: 2 * width, :]
    cross = total[3 * width : 4 * width, :]
    upper = jnp.concatenate([total[2 * width : 3 * width, :], cross], axis=1)
    lower = jnp.concatenate([cross.T, total[4 * width : 5 * width, :]], axis=1)
    whole = jnp.concatenate([upper, lower], axis=0)
    applied = dot(whole, sketched, precision=HIGHEST_PREC)
    gram = dot(sketched, applied, ((0,), (0,)), precision=HIGHEST_PREC)
    inverted = inverse_factor(gram)
    scale = math.sqrt(members * rows)
    weights = dot(sketched, inverted, ((1,), (1,)), precision=HIGHEST_PREC)
    left_high, left_low = halves(weights * scale)

    def out(at):
        here = pl.ds(at, PIECE)
        left_rows = left_cat[here, :]
        left_out[here, :] = (dot(left_rows, left_high) + dot(left_rows, left_low)).astype(BF16)

    pieces(rows, out)
    project = dot(applied, inverted, ((1,), (1,)), precision=HIGHEST_PREC)
    high, rest = halves(project / scale)
    project_high[...] = high
    project_low[...] = rest
    each(members, lambda d: scatter(d).wait_send())
    each(members, lambda d: spread(d).wait_send())


def panel_kernel(front_count, left, right, panel, inverse, panel_out, pivots, send, recv):
    leaf, front = lax.axis_index("leaf"), lax.axis_index("front")
    pivot_rows = inverse.shape[0]

    def device(d):
        return (leaf, lax.rem(front + d, front_count))

    greet((front_count, device))

    def share(d):
        return pltpu.make_async_remote_copy(
            src_ref=right.at[pl.ds(0, pivot_rows), :],
            dst_ref=pivots.at[front],
            send_sem=send.at[d],
            recv_sem=recv.at[d],
            device_id=device(d),
            device_id_type=MESH,
        )

    each(front_count, lambda d: share(d).start())
    pivots[front] = right[:pivot_rows, :]
    each(front_count, lambda d: share(d).wait_recv())
    right_piv = pivots[0]

    def out(at):
        here = pl.ds(at, PIECE)
        updated = panel[here, :].astype(F32) - dot(left[here, :], right_piv, ((1,), (1,)))
        high, rest = halves(updated)
        panel_out[here, :] = (dot(high, inverse[...]) + dot(rest, inverse[...])).astype(BF16)

    pieces(left.shape[0], out)
    each(front_count, lambda d: share(d).wait_send())


def call(kernel, outs, operands, scalars, scratch, flops, moved, **more):
    return pl.pallas_call(
        kernel,
        out_shape=outs,
        in_specs=[SMEM_SPEC] * scalars + [VMEM_SPEC] * (len(operands) - scalars),
        out_specs=tuple(VMEM_SPEC for _ in outs),
        scratch_shapes=scratch,
        compiler_params=pltpu.CompilerParams(vmem_limit_bytes=VMEM_LIMIT, **more),
        cost_estimate=pl.CostEstimate(flops=flops, bytes_accessed=moved, transcendentals=0),
    )(*operands)


def on_device(child_u, child_v, sketch, map_own, map_peer, live_rows, front_panel, pivot_inverse):
    rows, width = child_u.shape
    level_count = sketch.shape[0]
    front_count = lax.axis_size("front")
    left, right = child_u, child_v
    narrow = jax.ShapeDtypeStruct((rows, width), BF16)
    cat = jax.ShapeDtypeStruct((rows, 2 * width), BF16)
    small = jax.ShapeDtypeStruct((2 * width, width), BF16)
    pairs = [pltpu.VMEM((2 * rows, width), F32)] * 2
    singles = [pltpu.VMEM((rows, width), F32)] * 2
    unit = 22_000_000
    others = []
    for level in range(level_count):
        tail = jnp.broadcast_to(live_rows[level], (width,))
        others.append(from_partner(jnp.concatenate([map_peer[level], tail]), "leaf", level))
    left_sibling = from_partner(left, "leaf", 0)
    other_sketch = [from_partner(sketch[level], "leaf", level) for level in range(level_count)]
    for level in range(level_count):
        members = 2 ** (level + 1) * front_count
        chunk = -(-5 * width // (8 * members)) * 8
        live = live_rows[level].reshape(1, 1)
        if level:
            left_sibling = from_partner(left, "leaf", level)
        if level == 0:
            ahead = (others[0], other_sketch[0])
            right_sent, (others[0], other_sketch[0]) = lax.optimization_barrier((right, ahead))
        elif level == level_count - 1:
            right_sent, left_sibling = lax.optimization_barrier((right, left_sibling))
        else:
            right_sent = right
        right_sibling = from_partner(right_sent, "leaf", level)
        with jax.named_scope("own_rows"):
            left_own, right_own = call(
                own_kernel, (narrow, narrow), [map_own[level], live, left, right], 2, pairs,
                rows * width, unit,
            )
        with jax.named_scope("sketch_sums"):
            (sketch_sums,) = call(
                sketch_kernel, (jax.ShapeDtypeStruct((2 * width, width), F32),),
                [others[level], right, right_own, sketch[level], other_sketch[level]],
                1, singles, 4 * rows * width * width, unit,
            )
        with jax.named_scope("left_rows"):
            left_cat, gram_sums = call(
                left_kernel, (cat, jax.ShapeDtypeStruct((3 * width, width), F32)),
                [map_peer[level], live, left_sibling, left_own], 2, singles,
                8 * rows * width * width, unit,
            )
        if level == 0:
            (gram_sums, sketch_sums), others[2:], other_sketch[2:] = lax.optimization_barrier(
                ((gram_sums, sketch_sums), others[2:], other_sketch[2:])
            )
        with jax.named_scope("group_sum_and_factor"):
            left, project_high, project_low = call(
                functools.partial(factor_kernel, level, front_count),
                (narrow, small, small), [sketch_sums, gram_sums, left_cat], 0,
                [
                    pltpu.VMEM((members * chunk, width), F32),
                    pltpu.VMEM((members, chunk, width), F32),
                    pltpu.VMEM((chunk, width), F32),
                    pltpu.VMEM((members * chunk, width), F32),
                ]
                + [pltpu.SemaphoreType.DMA((members,))] * 4,
                8 * rows * width * width, 4 * unit,
                collective_id=level, has_side_effects=True,
            )
        if level == 0:
            (left, project_high), others[1:], other_sketch[1:] = lax.optimization_barrier(
                ((left, project_high), others[1:], other_sketch[1:])
            )
        with jax.named_scope("right_rows"):
            (right,) = call(
                right_kernel, (narrow,),
                [map_peer[level], live, right_sibling, right_own, project_high, project_low],
                2, singles, 8 * rows * width * width, unit,
            )
    with jax.named_scope("panel"):
        (panel_out,) = call(
            functools.partial(panel_kernel, front_count),
            (jax.ShapeDtypeStruct(front_panel.shape, BF16),),
            [left, right, front_panel, pivot_inverse], 0,
            [pltpu.VMEM((front_count,) + pivot_inverse.shape, BF16)]
            + [pltpu.SemaphoreType.DMA((front_count,))] * 2,
            8 * rows * width * width, unit,
            collective_id=level_count, has_side_effects=True,
        )
    return left, right, panel_out


def solution(mesh):
    placed = (
        P(("leaf", "front"), None),
        P(("leaf", "front"), None),
        P(None, ("leaf", "front"), None),
        P(None, ("leaf", "front")),
        P(None, ("leaf", "front")),
        P(None, ("leaf", "front")),
        P(("leaf", "front"), None),
        P("leaf", None),
    )
    return jax.shard_map(
        on_device,
        mesh=mesh,
        in_specs=placed,
        out_specs=(
            P(("leaf", "front"), None),
            P(("leaf", "front"), None),
            P(("leaf", "front"), None),
        ),
        check_vma=False,
    )
```
